256 devices in a mesh: arow: 8 (over z_hi, core), bcol: 32 (over y, x, z_lo).
Axes of the slice: x: 4, y: 4, z: 8 (z_hi: 4, z_lo: 2; z = z_hi * 2 + z_lo), core: 2. Of those that a mesh axis runs over, the one named last changes fastest.
Arguments:
- correlation: bfloat16 [2, 12, 4096, 4096], P(None, None, 'arow', 'bcol'), may hold values from -6 to 6
- freq_bins: int32 [12], replicated, may hold values from 1 to 1023
- coords_a: int32 [2, 4096], replicated, may hold values from 0 to 19999
- coords_b: int32 [2, 4096], replicated, may hold values from 0 to 19999
- assign_a: int32 [4096], P('arow'), may hold values from 0 to 4095, each once
- assign_b: int32 [4096], P('bcol'), may hold values from 0 to 4095, each once
- slow_a: int32 [2, 512], replicated, may hold values from -24 to 24
- slow_b: int32 [2, 512], replicated, may hold values from -24 to 24
Outputs:
- power: float32 [12, 512, 512], P(None, 'bcol', 'arow')
The draws below stay inside these ranges and needn't reach their ends.
All inputs are finite; a program needn't handle non-finite values.
Results may differ from the reference program's by a relative error of at most 0.0034.
Values sent between devices are 32-bit elements; how exact they have to be, the bound alone decides.
A program may use at most 128 MiB of HBM per device.

```python
import math
import jax
import jax.numpy as jnp
from jax import lax

NA = 4096
NB = 4096
P_SIZE = 512
F = 12


def set_ends(values, rng, smallest, top_value):
    spot = [jax.random.randint(jax.random.fold_in(rng, axis), (), 0, length) for axis, length in enumerate(values.shape)]
    main_axis = values.shape.index(max(values.shape))
    beside = spot[:main_axis] + [(spot[main_axis] + 1) % values.shape[main_axis]] + spot[main_axis + 1:]
    return values.at[tuple(spot)].set(smallest).at[tuple(beside)].set(top_value)


def steps_of(own_key, dims, cuts, low, top_value):
    factor_of, own = 1.0, jax.random.fold_in(own_key, 6)
    for axis_at, shards_of in cuts:
        heights = jnp.exp(jax.random.uniform(jax.random.fold_in(own, axis_at), (shards_of,), jnp.float32, low / len(cuts), top_value / len(cuts)))
        factor_of = factor_of * jnp.repeat(heights, dims[axis_at] // shards_of).reshape([-1 if axis == axis_at else 1 for axis in range(len(dims))])
    return factor_of


def bell_draw(stream_key, extent, scale, most, shards=(), kind=jnp.bfloat16):
    values = scale * jax.random.normal(stream_key, extent, jnp.float32)
    if shards:
        values = values * steps_of(stream_key, extent, shards, -0.22, 0.18)
    return jnp.clip(values, -most, most).astype(kind)


def setup_inputs(seed: int = 0) -> dict:
    key_of = jax.random.split(jax.random.key(seed), 9)
    return {
        "correlation": bell_draw(key_of[0], (2, F, NA, NB), 1.0, 6.0, ((2, 8), (3, 32))),
        "freq_bins": set_ends(jax.random.randint(key_of[1], (F,), 1, 1024), jax.random.fold_in(key_of[1], 1), 1, 1023).astype(jnp.int32),
        "coords_a": set_ends(jax.random.randint(key_of[2], (2, NA), 0, 20000), jax.random.fold_in(key_of[2], 1), 0, 19999).astype(jnp.int32),
        "coords_b": set_ends(jax.random.randint(key_of[3], (2, NB), 0, 20000), jax.random.fold_in(key_of[3], 1), 0, 19999).astype(jnp.int32),
        "assign_a": jax.random.permutation(key_of[4], NA).astype(jnp.int32),
        "assign_b": jax.random.permutation(key_of[5], NB).astype(jnp.int32),
        "slow_a": set_ends(jax.random.randint(key_of[6], (2, P_SIZE), -24, 25), jax.random.fold_in(key_of[6], 1), -24, 24).astype(jnp.int32),
        "slow_b": set_ends(jax.random.randint(key_of[7], (2, P_SIZE), -24, 25), jax.random.fold_in(key_of[7], 1), -24, 24).astype(jnp.int32),
    }


phase_modulus = 51200000


def steer(coords, assign, slow, freq, scale):
    place = jnp.take(coords, assign, axis=1)
    products = slow[0][:, None] * place[0][None, :] + slow[1][:, None] * place[1][None, :]
    turns = jnp.remainder(freq * products, phase_modulus)
    phase = turns.astype(jnp.float32) * jnp.float32(2.0 * math.pi / phase_modulus)
    real_part = (jnp.cos(phase) * scale).astype(jnp.bfloat16)
    imag_part = (-jnp.sin(phase) * scale).astype(jnp.bfloat16)
    return real_part, imag_part


def reference(correlation, freq_bins, coords_a, coords_b, assign_a, assign_b, slow_a, slow_b):
    def one_bin(index):
        freq = freq_bins[index]
        corr_re = correlation[0, index]
        corr_im = correlation[1, index]
        ua_re, ua_im = steer(coords_a, assign_a, slow_a, freq, NA ** -0.5)
        ub_re, ub_im = steer(coords_b, assign_b, slow_b, freq, NB ** -0.5)
        z_re = jnp.dot(corr_re, ub_re.T, preferred_element_type=jnp.float32) - jnp.dot(corr_im, ub_im.T, preferred_element_type=jnp.float32)
        z_im = jnp.dot(corr_re, ub_im.T, preferred_element_type=jnp.float32) + jnp.dot(corr_im, ub_re.T, preferred_element_type=jnp.float32)
        left_re = ua_re.astype(jnp.float32)
        left_im = ua_im.astype(jnp.float32)
        high = lax.Precision.HIGHEST
        y_re = jnp.dot(left_re, z_re, precision=high) + jnp.dot(left_im, z_im, precision=high)
        y_im = jnp.dot(left_re, z_im, precision=high) - jnp.dot(left_im, z_re, precision=high)
        return (y_re * y_re + y_im * y_im).T

    return lax.map(one_bin, jnp.arange(F, dtype=jnp.int32))
```

```python
import jax
import jax.numpy as jnp
from jax import lax
from jax.experimental import pallas as pl
from jax.experimental.pallas import tpu as pltpu
from jax.sharding import PartitionSpec as P

F = 12
ROUNDS = 3
LINE = 4
NZ = 8
MESH = pl.DeviceIdType.MESH

SIN = (4.442882834149931, -7.308241154546232, 3.6062889582237627, -0.8457635961366404, 0.10920575361787692)
COS = (1.4142134965650095, -6.978850988238499, 5.7394611706724765, -1.883562987243115, 0.3106981916942927)


def cos_sin(turns):
    r = turns.astype(jnp.float32) * jnp.float32(2.0**-32)
    u = r * r
    s = jnp.float32(SIN[4])
    c = jnp.float32(COS[4])
    for i in (3, 2, 1, 0):
        s = s * u + jnp.float32(SIN[i])
        c = c * u + jnp.float32(COS[i])
    s = s * r
    return 1.0 - s * s, s * c


def kernel(corr_hbm, xa_ref, sa_ref, xb_ref, sb_ref, out_ref,
           corr_v, rhs, cs_a, part, core_in, summed, line_in, coord_in,
           cs_b, v_hi, v_lo, y_part, y_in, z_out, z_in, f_out, f_in,
           corr_sem, core_ss, core_rs, line_ss, line_rs, coord_ss, coord_rs,
           y_ss, y_rs, z_ss, z_rs, f_ss, f_rs):
    arow = lax.axis_index("arow")
    bcol = lax.axis_index("bcol")
    core = arow % 2
    z = (arow // 2) * 2 + bcol % 2
    y = bcol // 8
    x = (bcol // 2) % 4
    g = x * (1 - core) + y * core
    h = y * (1 - core) + x * core

    def at(gg, hh, zz, cc_same=True):
        xx = gg * (1 - core) + hh * core
        yy = hh * (1 - core) + gg * core
        return ((zz // 2) * 2 + core, (yy * 4 + xx) * 2 + zz % 2)

    sibling = ((z // 2) * 2 + 1 - core, bcol)
    line_peer = [at((g + 1 + k) % LINE, h, z) for k in range(3)]
    y_peer = [at(g, (h + 1 + k) % LINE, z) for k in range(3)]
    z_peer = [at(g, h, (z + 1 + k) % NZ) for k in range(7)]

    loads = []
    for r in range(ROUNDS):
        cp = pltpu.make_async_copy(
            corr_hbm.at[:, pl.ds(r * 4, 4)], corr_v.at[:, pl.ds(r * 4, 4)], corr_sem.at[r]
        )
        cp.start()
        loads.append(cp)

    barrier = pltpu.get_barrier_semaphore()
    peers = [sibling] + line_peer + y_peer + z_peer
    for p in peers:
        pl.semaphore_signal(barrier, inc=1, device_id=p, device_id_type=MESH)
    pl.semaphore_wait(barrier, len(peers))

    def remote(src, dst, ss, rs, dev):
        return pltpu.make_async_remote_copy(
            src_ref=src, dst_ref=dst, send_sem=ss, recv_sem=rs, device_id=dev, device_id_type=MESH
        )

    def coord_copy(k):
        return remote(xb_ref.at[(g + 1 + k) % LINE], coord_in.at[k], coord_ss.at[k], coord_rs.at[k], line_peer[k])

    for k in range(3):
        coord_copy(k).start()

    def core_copy(s):
        return remote(part.at[s], core_in.at[s], core_ss.at[s], core_rs.at[s], sibling)

    def line_copy(r, k):
        return remote(
            summed.at[r * 4 + k], line_in.at[r * 3 + k], line_ss.at[r * 3 + k], line_rs.at[r * 3 + k], line_peer[k]
        )

    def a_side(b, half, dst):
        xs = xa_ref[b, 0:1, :]
        ys = xa_ref[b, 1:2, :]

        def steer(i, carry):
            rows = pl.ds(pl.multiple_of(i * 16, 16), 16)
            s0 = sa_ref[half, 0, rows, :]
            s1 = sa_ref[half, 1, rows, :]
            s0 = jnp.concatenate([s0] * 4, axis=1)
            s1 = jnp.concatenate([s1] * 4, axis=1)
            c, s = cos_sin(s0 * xs + s1 * ys)
            cs_a[rows, 0:512] = c.astype(jnp.bfloat16)
            cs_a[rows, 512:1024] = s.astype(jnp.bfloat16)
            return carry

        lax.fori_loop(0, 16, steer, 0)
        cr = corr_v[0, b]
        ci = corr_v[1, b]
        rhs[0:512, 0:128] = cr
        rhs[0:512, 128:256] = ci
        rhs[512:1024, 0:128] = -ci
        rhs[512:1024, 128:256] = cr
        dst[...] = jnp.dot(cs_a[...], rhs[...], preferred_element_type=jnp.float32)

    def finish(s):
        core_copy(s).wait_recv()
        summed[s] = summed[s] + core_in[s]

    def a_step(s, carry):
        r4 = (s // 4) * 4
        k = s % 4
        a_side(r4 + (h + 1 + k) % LINE, 1 - core, part.at[s])
        core_copy(s).start()
        a_side(r4 + (g + 1 + k) % LINE, core, summed.at[s])

        @pl.when(s > 0)
        def _():
            finish(s - 1)

            @pl.when(k > 0)
            def _():
                slot = (s // 4) * 3 + k - 1
                remote(
                    summed.at[s - 1], line_in.at[slot], line_ss.at[slot], line_rs.at[slot],
                    at((g + k) % LINE, h, z),
                ).start()

        return carry

    def b_steer(r):
        rows = [coord_in.at[0], coord_in.at[1], coord_in.at[2], xb_ref.at[g]]
        xs = jnp.concatenate([q[2 * r : 2 * r + 1, :] for q in rows], axis=1)
        ys = jnp.concatenate([q[2 * r + 1 : 2 * r + 2, :] for q in rows], axis=1)

        def steer(i, carry):
            rows = pl.ds(pl.multiple_of(i * 16, 16), 16)
            s0 = sb_ref[0, rows, :]
            s1 = sb_ref[1, rows, :]
            s0 = jnp.concatenate([s0] * 4, axis=1)
            s1 = jnp.concatenate([s1] * 4, axis=1)
            c, s = cos_sin(s0 * xs + s1 * ys)
            c = c.astype(jnp.bfloat16)
            s = s.astype(jnp.bfloat16)
            for k in range(4):
                cs_b[rows, k * 256 : k * 256 + 128] = c[:, k * 128 : k * 128 + 128]
                cs_b[rows, k * 256 + 128 : k * 256 + 256] = s[:, k * 128 : k * 128 + 128]
            return carry

        lax.fori_loop(0, 32, steer, 0)

    def y_copy(r, k):
        return remote(
            y_part.at[r, (h + 1 + k) % LINE], y_in.at[r * 3 + k], y_ss.at[r * 3 + k], y_rs.at[r * 3 + k], y_peer[k]
        )

    def b_side(r):
        b_steer(r)
        for k in range(4):
            if k < 3:
                line_copy(r, k).wait_recv()
            w = line_in[r * 3 + k] if k < 3 else summed[r * 4 + 3]
            hi = w.astype(jnp.bfloat16)
            lo = (w - hi.astype(jnp.float32)).astype(jnp.bfloat16)
            for dst, val in ((v_hi, hi), (v_lo, lo)):
                dst[0:256, k * 256 : k * 256 + 256] = val
                dst[256:512, k * 256 : k * 256 + 128] = val[:, 128:256]
                dst[256:512, k * 256 + 128 : k * 256 + 256] = -val[:, 0:128]

        for k in range(4):
            block = (h + 1 + k) % LINE
            steer = cs_b[pl.ds(pl.multiple_of(block * 128, 128), 128), :]
            dims = (((1,), (1,)), ((), ()))
            y_part[r, block] = lax.dot_general(
                steer, v_hi[...], dims, preferred_element_type=jnp.float32
            ) + lax.dot_general(steer, v_lo[...], dims, preferred_element_type=jnp.float32)
            if k < 3:
                y_copy(r, k).start()

    def z_copy(r, k):
        return remote(
            z_out.at[r, (z + 1 + k) % NZ], z_in.at[r * 7 + k], z_ss.at[r * 7 + k], z_rs.at[r * 7 + k], z_peer[k]
        )

    def z_send(r):
        for k in range(3):
            y_copy(r, k).wait_recv()
        t = y_part[r, h] + y_in[r * 3] + y_in[r * 3 + 1] + y_in[r * 3 + 2]
        for zh in range(4):
            for zl in range(2):
                piece = t[zl * 64 : zl * 64 + 64]
                z_out[r, zh * 2 + zl] = jnp.concatenate(
                    [piece[:, zh * 64 : zh * 64 + 64], piece[:, 256 + zh * 64 : 256 + zh * 64 + 64]], axis=1
                )
        for k in range(7):
            z_copy(r, k).start()

    def f_copy(r, k):
        return remote(
            f_out.at[r, (g + 1 + k) % LINE], f_in.at[r * 3 + k], f_ss.at[r * 3 + k], f_rs.at[r * 3 + k], line_peer[k]
        )

    def power(r):
        for k in range(7):
            z_copy(r, k).wait_recv()
        t = z_out[r, z]
        for k in range(7):
            t = t + z_in[r * 7 + k]
        t = t * jnp.float32(2.0**-12)
        t = t * t
        t = t + pltpu.roll(t, 64, 1)
        for i in range(4):
            f_out[r, i] = t[i * 16 : i * 16 + 16]
        for k in range(3):
            f_copy(r, k).start()
        out_ref[r * 4 + g] = f_out[r, g][:, 0:64]

    loads[0].wait()
    lax.fori_loop(0, 4, a_step, 0)
    loads[1].wait()
    lax.fori_loop(4, 8, a_step, 0)
    for k in range(3):
        coord_copy(k).wait_recv()
    b_side(0)
    loads[2].wait()
    lax.fori_loop(8, 12, a_step, 0)
    finish(11)
    b_side(1)
    z_send(0)
    b_side(2)
    z_send(1)
    power(0)
    z_send(2)
    power(1)
    power(2)
    for r in range(ROUNDS):
        for k in range(3):
            f_copy(r, k).wait_recv()
            out_ref[r * 4 + (g + 3 - k) % LINE] = f_in[r * 3 + k][:, 0:64]

    def drain_core(s, carry):
        core_copy(s).wait_send()
        return carry

    lax.fori_loop(0, F, drain_core, 0)
    for k in range(3):
        coord_copy(k).wait_send()
    for r in range(ROUNDS):
        for k in range(3):
            line_copy(r, k).wait_send()
            y_copy(r, k).wait_send()
            f_copy(r, k).wait_send()
        for k in range(7):
            z_copy(r, k).wait_send()


def fractions(freq, coords, assign):
    place = jnp.take(coords, assign, axis=1)
    product = freq[:, None, None] * place[None]
    whole = product // 3125
    rest = product - whole * 3125
    return (whole << 18) + (rest << 18) // 3125


def body(correlation, freq_bins, coords_a, coords_b, assign_a, assign_b, slow_a, slow_b):
    core = lax.axis_index("arow") % 2
    xa = fractions(freq_bins, coords_a, assign_a)
    xb = fractions(freq_bins, coords_b, assign_b)
    xb = xb.reshape(ROUNDS, LINE, 2, 128).transpose(1, 0, 2, 3).reshape(LINE, ROUNDS * 2, 128)
    xb = jnp.pad(xb, ((0, 0), (0, 2), (0, 0)))
    sa = slow_a.reshape(2, 4, 2, 64).transpose(2, 0, 1, 3).reshape(2, 2, 256)
    sa = jnp.broadcast_to(sa[..., None], (2, 2, 256, 128))
    sb = slow_b.reshape(2, 4, 4, 2, 16)
    sb = jnp.where(core == 0, sb.transpose(0, 1, 3, 2, 4).reshape(2, 512), sb.transpose(0, 2, 3, 1, 4).reshape(2, 512))
    sb = jnp.broadcast_to(sb[..., None], (2, 512, 128))

    f32, bf16 = jnp.float32, jnp.bfloat16
    vmem = pl.BlockSpec(memory_space=pltpu.VMEM)
    dma = pltpu.SemaphoreType.DMA
    return pl.pallas_call(
        kernel,
        out_shape=jax.ShapeDtypeStruct((F, 16, 64), f32),
        in_specs=[pl.BlockSpec(memory_space=pl.ANY), vmem, vmem, vmem, vmem],
        out_specs=vmem,
        scratch_shapes=[
            pltpu.VMEM((2, F, 512, 128), bf16),
            pltpu.VMEM((1024, 256), bf16),
            pltpu.VMEM((256, 1024), bf16),
            pltpu.VMEM((F, 256, 256), f32),
            pltpu.VMEM((F, 256, 256), f32),
            pltpu.VMEM((F, 256, 256), f32),
            pltpu.VMEM((9, 256, 256), f32),
            pltpu.VMEM((3, 8, 128), jnp.int32),
            pltpu.VMEM((512, 1024), bf16),
            pltpu.VMEM((512, 1024), bf16),
            pltpu.VMEM((512, 1024), bf16),
            pltpu.VMEM((ROUNDS, LINE, 128, 512), f32),
            pltpu.VMEM((9, 128, 512), f32),
            pltpu.VMEM((ROUNDS, NZ, 64, 128), f32),
            pltpu.VMEM((21, 64, 128), f32),
            pltpu.VMEM((ROUNDS, LINE, 16, 128), f32),
            pltpu.VMEM((9, 16, 128), f32),
            dma((3,)),
            dma((F,)), dma((F,)),
            dma((9,)), dma((9,)),
            dma((3,)), dma((3,)),
            dma((9,)), dma((9,)),
            dma((21,)), dma((21,)),
            dma((9,)), dma((9,)),
        ],
        compiler_params=pltpu.CompilerParams(
            collective_id=0, has_side_effects=True, vmem_limit_bytes=56 * 2**20
        ),
        cost_estimate=pl.CostEstimate(flops=7 * 10**9, bytes_accessed=4 * 10**6, transcendentals=0),
    )(correlation, xa, sa, xb, sb)


def solution(mesh):
    return jax.shard_map(
        body,
        mesh=mesh,
        in_specs=(P(None, None, "arow", "bcol"), P(), P(), P(), P("arow"), P("bcol"), P(), P()),
        out_specs=P(None, "bcol", "arow"),
        check_vma=False,
    )
```

```python
import jax
import jax.numpy as jnp
from jax import lax
from jax.experimental import pallas as pl
from jax.experimental.pallas import tpu as pltpu
from jax.sharding import PartitionSpec as P

F = 12
ROUNDS = 3
UNITS = 6
LINE = 4
NZ = 8
MESH = pl.DeviceIdType.MESH

SIN = (4.442882834149931, -7.308241154546232, 3.6062889582237627, -0.8457635961366404, 0.10920575361787692)
COS = (1.4142134965650095, -6.978850988238499, 5.7394611706724765, -1.883562987243115, 0.3106981916942927)


def cos_sin(turns):
    r = turns.astype(jnp.float32) * jnp.float32(2.0**-32)
    u = r * r
    s = jnp.float32(SIN[4])
    c = jnp.float32(COS[4])
    for i in (3, 2, 1, 0):
        s = s * u + jnp.float32(SIN[i])
        c = c * u + jnp.float32(COS[i])
    s = s * r
    return 1.0 - s * s, s * c


def fraction(freq, place):
    product = freq * place
    return product * 83 + (product.astype(jnp.float32) * jnp.float32(0.88608)).astype(jnp.int32)


def places(coords_ref, assign, grid):
    for i in range(32):
        grid[2 * i : 2 * i + 2, :] = coords_ref[:, i * 128 : i * 128 + 128]
    table = grid[...]
    high = (table >> 8).astype(jnp.float32).astype(jnp.bfloat16)
    low = (table & 255).astype(jnp.float32).astype(jnp.bfloat16)
    n = assign.shape[1]
    lane = lax.broadcasted_iota(jnp.int32, (128, n), 0)
    pick = jnp.where(lane == (assign & 127), 1.0, 0.0).astype(jnp.bfloat16)
    value = 256.0 * jnp.dot(high, pick, preferred_element_type=jnp.float32) + jnp.dot(
        low, pick, preferred_element_type=jnp.float32
    )
    row = lax.broadcasted_iota(jnp.int32, (64, n), 0)
    value = jnp.where((row >> 1) == (assign >> 7), value, 0.0)
    px = jnp.sum(jnp.where((row & 1) == 0, value, 0.0), axis=0, keepdims=True)
    py = jnp.sum(jnp.where((row & 1) == 1, value, 0.0), axis=0, keepdims=True)
    return px.astype(jnp.int32), py.astype(jnp.int32)


def columns(slow_row):
    wide = jnp.broadcast_to(slow_row.astype(jnp.float32), (128, 128)).astype(jnp.bfloat16)
    i = lax.broadcasted_iota(jnp.int32, (128, 128), 0)
    j = lax.broadcasted_iota(jnp.int32, (128, 128), 1)
    eye = jnp.where(i == j, 1.0, 0.0).astype(jnp.bfloat16)
    out = lax.dot_general(eye, wide, (((1,), (1,)), ((), ())), preferred_element_type=jnp.float32)
    return out.astype(jnp.int32)


def kernel(corr_hbm, freq_ref, coords_a_ref, coords_b_ref, assign_a_ref, assign_b_ref, slow_a_ref, slow_b_ref, out_ref,
           corr_v, grid_a, grid_b, place_a, place_b, sa, sb, rhs, cs_a, part, core_in, line_in, coord_in,
           cs_b, v_hi, v_lo, y_part, y_in1, y_fwd, y_in2, z_out, z_in, f_out, f_in,
           corr_sem, core_ss, core_rs, line_ss, line_rs, coord_ss, coord_rs,
           y1_ss, y1_rs, y2_ss, y2_rs, z_ss, z_rs, f_ss, f_rs):
    arow = lax.axis_index("arow")
    bcol = lax.axis_index("bcol")
    core = arow % 2
    z = (arow // 2) * 2 + bcol % 2
    y = bcol // 8
    x = (bcol // 2) % 4
    g = x * (1 - core) + y * core
    h = y * (1 - core) + x * core

    def at(gg, hh, zz):
        xx = gg * (1 - core) + hh * core
        yy = hh * (1 - core) + gg * core
        return ((zz // 2) * 2 + core, (yy * 4 + xx) * 2 + zz % 2)

    near = h + 1 - 2 * (h % 2)
    wrap = 3 - h
    diagonal = 3 - near
    sibling = ((z // 2) * 2 + 1 - core, bcol)
    line_peer = [at((g + 1 + k) % LINE, h, z) for k in range(3)]
    z_peer = [at(g, h, (z + 1 + k) % NZ) for k in range(7)]

    loads = []
    for r in range(ROUNDS):
        cp = pltpu.make_async_copy(
            corr_hbm.at[:, pl.ds(r * 4, 4)], corr_v.at[:, pl.ds(r * 4, 4)], corr_sem.at[r]
        )
        cp.start()
        loads.append(cp)

    barrier = pltpu.get_barrier_semaphore()
    peers = [sibling, at(g, near, z), at(g, wrap, z)] + line_peer + z_peer
    for p in peers:
        pl.semaphore_signal(barrier, inc=1, device_id=p, device_id_type=MESH)

    bx, by = places(coords_b_ref, assign_b_ref[...], grid_b)
    place_b[...] = jnp.zeros_like(place_b)
    place_b[0:1, :] = bx
    place_b[1:2, :] = by
    ax, ay = places(coords_a_ref, assign_a_ref[...], grid_a)
    place_a[0:1, :] = ax
    place_a[1:2, :] = ay
    for i in range(2):
        for t in range(4):
            c = columns(slow_a_ref[i : i + 1, t * 128 : t * 128 + 128])
            sa[i, t * 64 : t * 64 + 64, :] = c[0:64]
            sa[i, 256 + t * 64 : 256 + t * 64 + 64, :] = c[64:128]
            c = columns(slow_b_ref[i : i + 1, t * 128 : t * 128 + 128])
            for xx in range(4):
                gg = xx * (1 - core) + t * core
                hh = t * (1 - core) + xx * core
                for zl in range(2):
                    for half in range(2):
                        src = (xx * 2 + zl) * 16 + half * 8
                        dst = pl.multiple_of(half * 256 + hh * 64 + zl * 32 + gg * 8, 8)
                        sb[i, pl.ds(dst, 8), :] = c[src : src + 8]

    pl.semaphore_wait(barrier, len(peers))

    def remote(src, dst, ss, rs, dev):
        return pltpu.make_async_remote_copy(
            src_ref=src, dst_ref=dst, send_sem=ss, recv_sem=rs, device_id=dev, device_id_type=MESH
        )

    def coord_copy(k):
        return remote(place_b, coord_in.at[k], coord_ss.at[k], coord_rs.at[k], line_peer[k])

    for k in range(3):
        coord_copy(k).start()

    def core_copy(s):
        return remote(part.at[s, 1 - core], core_in.at[s], core_ss.at[s], core_rs.at[s], sibling)

    def line_copy(s, slot, rel):
        return remote(
            part.at[s, core], line_in.at[slot], line_ss.at[slot], line_rs.at[slot], at((g + rel) % LINE, h, z)
        )

    def steer_rows(s_ref, xs, ys, put):
        def steer(i, carry):
            rows = pl.ds(pl.multiple_of(i * 16, 16), 16)
            s0 = s_ref[0, rows, :]
            s1 = s_ref[1, rows, :]
            s0 = jnp.concatenate([s0] * 4, axis=1)
            s1 = jnp.concatenate([s1] * 4, axis=1)
            c, s = cos_sin(s0 * xs + s1 * ys)
            put(rows, c.astype(jnp.bfloat16), s.astype(jnp.bfloat16))
            return carry

        lax.fori_loop(0, 32, steer, 0, unroll=4)

    def a_step(s, carry):
        k = s % 4
        b = (s // 4) * 4 + (x + y + 1 + k) % LINE
        freq = freq_ref[b]

        def put(rows, c, s_):
            cs_a[rows, 0:512] = c
            cs_a[rows, 512:1024] = s_

        steer_rows(sa, fraction(freq, place_a[0:1, :]), fraction(freq, place_a[1:2, :]), put)
        cr = corr_v[0, b]
        ci = corr_v[1, b]
        rhs[0:512, 0:128] = cr
        rhs[0:512, 128:256] = ci
        rhs[512:1024, 0:128] = -ci
        rhs[512:1024, 128:256] = cr
        w = jnp.dot(cs_a[...], rhs[...], preferred_element_type=jnp.float32)
        part[s, 0] = w[0:256]
        part[s, 1] = w[256:512]
        core_copy(s).start()

        @pl.when(s > 0)
        def _():
            finish(s - 1)

        return carry

    def finish(s):
        core_copy(s).wait_recv()
        part[s, core] = part[s, core] + core_in[s]
        rel = (h + 1 + s % 4) % LINE

        @pl.when(rel > 0)
        def _():
            line_copy(s, (s // 4) * 3 + rel - 1, rel).start()

    def b_steer(r):
        rows = [coord_in.at[0], coord_in.at[1], coord_in.at[2], place_b]
        freq = freq_ref[r * 4 + g]
        xs = fraction(freq, jnp.concatenate([q[0:1, :] for q in rows], axis=1))
        ys = fraction(freq, jnp.concatenate([q[1:2, :] for q in rows], axis=1))

        def put(rows, c, s):
            for k in range(4):
                cs_b[rows, k * 256 : k * 256 + 128] = c[:, k * 128 : k * 128 + 128]
                cs_b[rows, k * 256 + 128 : k * 256 + 256] = s[:, k * 128 : k * 128 + 128]

        steer_rows(sb, xs, ys, put)

    def pair(half):
        return (near, wrap) if half == 0 else (wrap, near)

    def y1_copy(u, j):
        first, _ = pair(u % 2)
        block = diagonal if j == 0 else first
        return remote(
            y_part.at[u, block], y_in1.at[u, j], y1_ss.at[u * 2 + j], y1_rs.at[u * 2 + j], at(g, first, z)
        )

    def y2_copy(u):
        _, second = pair(u % 2)
        return remote(y_fwd.at[u], y_in2.at[u], y2_ss.at[u], y2_rs.at[u], at(g, second, z))

    def b_side(r):
        b_steer(r)
        for k in range(4):
            if k < 3:
                line_copy(0, r * 3 + k, k + 1).wait_recv()
            w = line_in[r * 3 + k] if k < 3 else part[r * 4 + 3 - h, core]
            hi = w.astype(jnp.bfloat16)
            lo = (w - hi.astype(jnp.float32)).astype(jnp.bfloat16)
            for dst, val in ((v_hi, hi), (v_lo, lo)):
                dst[0:256, k * 256 : k * 256 + 256] = val
                dst[256:512, k * 256 : k * 256 + 128] = val[:, 128:256]
                dst[256:512, k * 256 + 128 : k * 256 + 256] = -val[:, 0:128]

        dims = (((1,), (1,)), ((), ()))
        for half in range(2):
            u = r * 2 + half
            steer = cs_b[half * 256 : half * 256 + 256, :]
            v = lax.dot_general(steer, v_hi[...], dims, preferred_element_type=jnp.float32)
            v = v + lax.dot_general(steer, v_lo[...], dims, preferred_element_type=jnp.float32)
            for i in range(4):
                y_part[u, i] = v[i * 64 : i * 64 + 64]
            for j in range(2):
                y1_copy(u, j).start()

    def y_forward(u):
        _, second = pair(u % 2)
        y1_copy(u, 0).wait_recv()
        y_fwd[u] = y_part[u, second] + y_in1[u, 0]
        y2_copy(u).start()

    def z_copy(u, k):
        return remote(
            z_out.at[u, (z + 1 + k) % NZ], z_in.at[u * 7 + k], z_ss.at[u * 7 + k], z_rs.at[u * 7 + k], z_peer[k]
        )

    def z_send(u):
        y1_copy(u, 1).wait_recv()
        y2_copy(u).wait_recv()
        t = y_part[u, h] + y_in1[u, 1] + y_in2[u]
        for zh in range(4):
            for zl in range(2):
                piece = t[zl * 32 : zl * 32 + 32]
                z_out[u, zh * 2 + zl] = jnp.concatenate(
                    [piece[:, zh * 64 : zh * 64 + 64], piece[:, 256 + zh * 64 : 256 + zh * 64 + 64]], axis=1
                )
        for k in (3, 2, 4, 1, 5, 0, 6):
            z_copy(u, k).start()

    def f_copy(u, k):
        return remote(
            f_out.at[u, (g + 1 + k) % LINE], f_in.at[u * 3 + k], f_ss.at[u * 3 + k], f_rs.at[u * 3 + k], line_peer[k]
        )

    def power(u):
        for k in range(7):
            z_copy(u, k).wait_recv()
        t = z_out[u, z]
        for k in range(7):
            t = t + z_in[u * 7 + k]
        t = t * jnp.float32(2.0**-12)
        t = t * t
        t = t + pltpu.roll(t, 64, 1)
        for i in range(4):
            f_out[u, i] = t[i * 8 : i * 8 + 8]
        for k in range(3):
            f_copy(u, k).start()
        out_ref[(u // 2) * 4 + g, (u % 2) * 8 : (u % 2) * 8 + 8, :] = f_out[u, g][:, 0:64]

    def each(fn, *units):
        for u in units:
            fn(u)

    loads[0].wait()
    lax.fori_loop(0, 4, a_step, 0)
    loads[1].wait()
    lax.fori_loop(4, 8, a_step, 0)
    for k in range(3):
        coord_copy(k).wait_recv()
    b_side(0)
    loads[2].wait()
    lax.fori_loop(8, 12, a_step, 0)
    finish(11)
    each(y_forward, 0, 1)
    b_side(1)
    each(z_send, 0, 1)
    each(y_forward, 2, 3)
    b_side(2)
    each(z_send, 2, 3)
    each(power, 0, 1)
    each(y_forward, 4, 5)
    each(power, 2, 3)
    each(z_send, 4, 5)
    each(power, 4, 5)
    for u in range(UNITS):
        for k in range(3):
            f_copy(u, k).wait_recv()
            out_ref[(u // 2) * 4 + (g + 3 - k) % LINE, (u % 2) * 8 : (u % 2) * 8 + 8, :] = f_in[u * 3 + k][:, 0:64]

    def drain_core(s, carry):
        core_copy(s).wait_send()
        return carry

    lax.fori_loop(0, F, drain_core, 0)
    for k in range(3):
        coord_copy(k).wait_send()
    for slot in range(9):
        line_copy(0, slot, slot % 3 + 1).wait_send()
    for u in range(UNITS):
        for j in range(2):
            y1_copy(u, j).wait_send()
        y2_copy(u).wait_send()
        for k in range(7):
            z_copy(u, k).wait_send()
        for k in range(3):
            f_copy(u, k).wait_send()


def body(correlation, freq_bins, coords_a, coords_b, assign_a, assign_b, slow_a, slow_b):
    i32, f32, bf16 = jnp.int32, jnp.float32, jnp.bfloat16
    vmem = pl.BlockSpec(memory_space=pltpu.VMEM)
    dma = pltpu.SemaphoreType.DMA
    return pl.pallas_call(
        kernel,
        out_shape=jax.ShapeDtypeStruct((F, 16, 64), f32),
        in_specs=[pl.BlockSpec(memory_space=pl.ANY), pl.BlockSpec(memory_space=pltpu.SMEM)] + [vmem] * 6,
        out_specs=vmem,
        scratch_shapes=[
            pltpu.VMEM((2, F, 512, 128), bf16),
            pltpu.VMEM((64, 128), i32),
            pltpu.VMEM((64, 128), i32),
            pltpu.VMEM((8, 512), i32),
            pltpu.VMEM((8, 128), i32),
            pltpu.VMEM((2, 512, 128), i32),
            pltpu.VMEM((2, 512, 128), i32),
            pltpu.VMEM((1024, 256), bf16),
            pltpu.VMEM((512, 1024), bf16),
            pltpu.VMEM((F, 2, 256, 256), f32),
            pltpu.VMEM((F, 256, 256), f32),
            pltpu.VMEM((9, 256, 256), f32),
            pltpu.VMEM((3, 8, 128), i32),
            pltpu.VMEM((512, 1024), bf16),
            pltpu.VMEM((512, 1024), bf16),
            pltpu.VMEM((512, 1024), bf16),
            pltpu.VMEM((UNITS, LINE, 64, 512), f32),
            pltpu.VMEM((UNITS, 2, 64, 512), f32),
            pltpu.VMEM((UNITS, 64, 512), f32),
            pltpu.VMEM((UNITS, 64, 512), f32),
            pltpu.VMEM((UNITS, NZ, 32, 128), f32),
            pltpu.VMEM((UNITS * 7, 32, 128), f32),
            pltpu.VMEM((UNITS, LINE, 8, 128), f32),
            pltpu.VMEM((UNITS * 3, 8, 128), f32),
            dma((3,)),
            dma((F,)), dma((F,)),
            dma((9,)), dma((9,)),
            dma((3,)), dma((3,)),
            dma((12,)), dma((12,)),
            dma((UNITS,)), dma((UNITS,)),
            dma((UNITS * 7,)), dma((UNITS * 7,)),
            dma((UNITS * 3,)), dma((UNITS * 3,)),
        ],
        compiler_params=pltpu.CompilerParams(
            collective_id=0, has_side_effects=True, vmem_limit_bytes=56 * 2**20
        ),
        cost_estimate=pl.CostEstimate(flops=7 * 10**9, bytes_accessed=4 * 10**6, transcendentals=0),
    )(correlation, freq_bins, coords_a, coords_b, assign_a.reshape(1, 512), assign_b.reshape(1, 128), slow_a, slow_b)


def solution(mesh):
    return jax.shard_map(
        body,
        mesh=mesh,
        in_specs=(P(None, None, "arow", "bcol"), P(), P(), P(), P("arow"), P("bcol"), P(), P()),
        out_specs=P(None, "bcol", "arow"),
        check_vma=False,
    )
```

```python
import jax
import jax.numpy as jnp
from jax import lax
from jax.experimental import pallas as pl
from jax.experimental.pallas import tpu as pltpu
from jax.sharding import PartitionSpec as P

F = 12
ROUNDS = 3
UNITS = 6
LINE = 4
NZ = 8
MESH = pl.DeviceIdType.MESH

SIN = (4.442882834149931, -7.308241154546232, 3.6062889582237627, -0.8457635961366404, 0.10920575361787692)
COS = (1.4142134965650095, -6.978850988238499, 5.7394611706724765, -1.883562987243115, 0.3106981916942927)


def cos_sin(turns):
    r = turns.astype(jnp.float32) * jnp.float32(2.0**-32)
    u = r * r
    s = jnp.float32(SIN[4])
    c = jnp.float32(COS[4])
    for i in (3, 2, 1, 0):
        s = s * u + jnp.float32(SIN[i])
        c = c * u + jnp.float32(COS[i])
    s = s * r
    return 1.0 - s * s, s * c


def fraction(freq, place):
    product = freq * place
    return product * 83 + (product.astype(jnp.float32) * jnp.float32(0.88608)).astype(jnp.int32)


def places(coords_ref, assign, grid):
    for i in range(32):
        grid[2 * i : 2 * i + 2, :] = coords_ref[:, i * 128 : i * 128 + 128]
    table = grid[...]
    high = (table >> 8).astype(jnp.float32).astype(jnp.bfloat16)
    low = (table & 255).astype(jnp.float32).astype(jnp.bfloat16)
    n = assign.shape[1]
    lane = lax.broadcasted_iota(jnp.int32, (128, n), 0)
    pick = jnp.where(lane == (assign & 127), 1.0, 0.0).astype(jnp.bfloat16)
    value = 256.0 * jnp.dot(high, pick, preferred_element_type=jnp.float32) + jnp.dot(
        low, pick, preferred_element_type=jnp.float32
    )
    row = lax.broadcasted_iota(jnp.int32, (64, n), 0)
    value = jnp.where((row >> 1) == (assign >> 7), value, 0.0)
    px = jnp.sum(jnp.where((row & 1) == 0, value, 0.0), axis=0, keepdims=True)
    py = jnp.sum(jnp.where((row & 1) == 1, value, 0.0), axis=0, keepdims=True)
    return px.astype(jnp.int32), py.astype(jnp.int32)


def columns(slow_row):
    wide = jnp.broadcast_to(slow_row.astype(jnp.float32), (128, 128)).astype(jnp.bfloat16)
    i = lax.broadcasted_iota(jnp.int32, (128, 128), 0)
    j = lax.broadcasted_iota(jnp.int32, (128, 128), 1)
    eye = jnp.where(i == j, 1.0, 0.0).astype(jnp.bfloat16)
    out = lax.dot_general(eye, wide, (((1,), (1,)), ((), ())), preferred_element_type=jnp.float32)
    return out.astype(jnp.int32)


def kernel(corr_hbm, freq_ref, coords_a_ref, coords_b_ref, assign_a_ref, assign_b_ref, slow_a_ref, slow_b_ref, out_ref,
           corr_v, grid_a, grid_b, place_a, place_b, sa, sb, rhs, cs_0, cs_1, cs_2, cs_3, turns_0, turns_1, turns_2, turns_3, part, core_in, line_in, coord_in,
           v_hi, v_lo, y_part, y_in1, y_fwd, y_in2, z_out, z_in, f_out, f_in,
           corr_sem, core_ss, core_rs, line_ss, line_rs, coord_ss, coord_rs,
           y1_ss, y1_rs, y2_ss, y2_rs, z_ss, z_rs, f_ss, f_rs):
    arow = lax.axis_index("arow")
    bcol = lax.axis_index("bcol")
    core = arow % 2
    z = (arow // 2) * 2 + bcol % 2
    y = bcol // 8
    x = (bcol // 2) % 4
    g = x * (1 - core) + y * core
    h = y * (1 - core) + x * core

    def at(gg, hh, zz):
        xx = gg * (1 - core) + hh * core
        yy = hh * (1 - core) + gg * core
        return ((zz // 2) * 2 + core, (yy * 4 + xx) * 2 + zz % 2)

    near = h + 1 - 2 * (h % 2)
    wrap = 3 - h
    diagonal = 3 - near
    sibling = ((z // 2) * 2 + 1 - core, bcol)
    line_peer = [at((g + 1 + k) % LINE, h, z) for k in range(3)]
    z_peer = [at(g, h, (z + 1 + k) % NZ) for k in range(7)]

    def each(fn, *units):
        for u in units:
            fn(u)

    def load(r):
        four = pl.ds(r * 4, 4)
        return pltpu.make_async_copy(corr_hbm.at[:, four], corr_v.at[:, four], corr_sem.at[r])

    for r in range(ROUNDS):
        load(r).start()

    barrier = pltpu.get_barrier_semaphore()
    peers = [sibling, at(g, near, z), at(g, wrap, z)] + line_peer + z_peer
    for p in peers:
        pl.semaphore_signal(barrier, inc=1, device_id=p, device_id_type=MESH)

    bx, by = places(coords_b_ref, assign_b_ref[...], grid_b)
    place_b[...] = jnp.zeros_like(place_b)
    place_b[0:1, :] = bx
    place_b[1:2, :] = by
    ax, ay = places(coords_a_ref, assign_a_ref[...], grid_a)
    place_a[...] = jnp.zeros_like(place_a)
    place_a[0:1, :] = ax
    place_a[1:2, :] = ay
    for i in range(2):
        for t in range(4):
            c = columns(slow_a_ref[i : i + 1, t * 128 : t * 128 + 128])
            sa[i, t * 64 : t * 64 + 64, :] = c[0:64]
            sa[i, 256 + t * 64 : 256 + t * 64 + 64, :] = c[64:128]
            c = columns(slow_b_ref[i : i + 1, t * 128 : t * 128 + 128])
            for xx in range(4):
                gg = xx * (1 - core) + t * core
                hh = t * (1 - core) + xx * core
                for zl in range(2):
                    for half in range(2):
                        src = (xx * 2 + zl) * 16 + half * 8
                        dst = pl.multiple_of(half * 256 + hh * 64 + zl * 32 + gg * 8, 8)
                        sb[i, pl.ds(dst, 8), :] = c[src : src + 8]

    def remote(src, dst, ss, rs, dev):
        return pltpu.make_async_remote_copy(
            src_ref=src, dst_ref=dst, send_sem=ss, recv_sem=rs, device_id=dev, device_id_type=MESH
        )

    def coord_copy(k):
        return remote(place_b, coord_in.at[k], coord_ss.at[k], coord_rs.at[k], line_peer[k])

    def core_copy(s):
        return remote(part.at[s, 1 - core], core_in.at[s], core_ss.at[s], core_rs.at[s], sibling)

    def line_copy(s, slot, rel):
        return remote(
            part.at[s, core], line_in.at[slot], line_ss.at[slot], line_rs.at[slot], at((g + rel) % LINE, h, z)
        )

    def steer(start, count, spec, cs):
        s_ref, turns = spec
        xs = turns[0:1, :]
        ys = turns[1:2, :]
        for t in range(0, count, 16):
            rows = pl.ds(pl.multiple_of(start + t, 16), 16)
            s0 = s_ref[0, rows, :]
            s1 = s_ref[1, rows, :]
            s0 = jnp.concatenate([s0] * 4, axis=1)
            s1 = jnp.concatenate([s1] * 4, axis=1)
            c, s = cos_sin(s0 * xs + s1 * ys)
            cs[rows, 0:512] = c.astype(jnp.bfloat16)
            cs[rows, 512:1024] = s.astype(jnp.bfloat16)

    def a_bin(s):
        return (s // 4) * 4 + (x + y + 1 + s % 4) % LINE

    def a_spec(s, turns):
        turns[...] = fraction(freq_ref[a_bin(s)], place_a[...])
        return sa, turns

    def b_spec(r, turns):
        rows = [coord_in.at[0], coord_in.at[1], coord_in.at[2], place_b]
        turns[...] = fraction(freq_ref[r * 4 + g], jnp.concatenate([q[...] for q in rows], axis=1))
        return sb, turns

    def a_dots(s, cs, spec, cs_next):
        b = a_bin(s)
        cr = corr_v[0, b]
        ci = corr_v[1, b]
        rhs[0:512, 0:128] = cr
        rhs[0:512, 128:256] = ci
        rhs[512:1024, 0:128] = -ci
        rhs[512:1024, 128:256] = cr

        w = jnp.dot(cs[...], rhs[...], preferred_element_type=jnp.float32)
        part[s, 0] = w[0:256]
        part[s, 1] = w[256:512]
        steer(0, 512, spec, cs_next)

    def finish(s):
        core_copy(s).wait_recv()
        part[s, core] = part[s, core] + core_in[s]
        rel = (h + 1 + s % 4) % LINE

        @pl.when(rel > 0)
        def _():
            slot = (s // 4) * 3 + rel - 1

            line_copy(s, slot, rel).start()

    def pair(d):
        return (near, wrap) if d == 0 else (wrap, near)

    def y1_copy(u, d, j):
        first, _ = pair(d)
        block = diagonal if j == 0 else first
        i = (u * 2 + d) * 2 + j
        return remote(y_part.at[u, d, block], y_in1.at[u, d, j], y1_ss.at[i], y1_rs.at[i], at(g, first, z))

    def y2_copy(u, d):
        _, second = pair(d)
        return remote(y_fwd.at[u, d], y_in2.at[u, d], y2_ss.at[u * 2 + d], y2_rs.at[u * 2 + d], at(g, second, z))

    def b_side(r, cs, spec, cs_next):
        for k in range(4):
            if k < 3:
                line_copy(0, r * 3 + k, k + 1).wait_recv()
            w = line_in[r * 3 + k] if k < 3 else part[r * 4 + 3 - h, core]
            hi = w.astype(jnp.bfloat16)
            lo = (w - hi.astype(jnp.float32)).astype(jnp.bfloat16)
            re, im = slice(k * 128, k * 128 + 128), slice(512 + k * 128, 512 + k * 128 + 128)
            for dst, val in ((v_hi, hi), (v_lo, lo)):
                dst[0:256, re] = val[:, 0:128]
                dst[0:256, im] = val[:, 128:256]
                dst[256:512, re] = val[:, 128:256]
                dst[256:512, im] = -val[:, 0:128]

        dims = (((1,), (1,)), ((), ()))
        for d in range(2):
            part_d = slice(d * 256, d * 256 + 256)
            v = lax.dot_general(cs[...], v_hi[part_d, :], dims, preferred_element_type=jnp.float32)
            v = v + lax.dot_general(cs[...], v_lo[part_d, :], dims, preferred_element_type=jnp.float32)
            for half in range(2):
                for i in range(4):
                    y_part[r * 2 + half, d, i] = v[half * 256 + i * 64 : half * 256 + i * 64 + 64]
        if spec is not None:
            steer(0, 512, spec, cs_next)
        for half in range(2):
            for d in range(2):
                for j in range(2):
                    y1_copy(r * 2 + half, d, j).start()

    def y_forward(u):
        for d in range(2):
            _, second = pair(d)
            y1_copy(u, d, 0).wait_recv()
            y_fwd[u, d] = y_part[u, d, second] + y_in1[u, d, 0]
            y2_copy(u, d).start()

    def z_copy(u, k):
        return remote(
            z_out.at[u, (z + 1 + k) % NZ], z_in.at[u * 7 + k], z_ss.at[u * 7 + k], z_rs.at[u * 7 + k], z_peer[k]
        )

    def z_send(u):
        t = []
        for d in range(2):
            y1_copy(u, d, 1).wait_recv()
            y2_copy(u, d).wait_recv()
            t.append(y_part[u, d, h] + y_in1[u, d, 1] + y_in2[u, d])
        for zh in range(4):
            for zl in range(2):
                z_out[u, zh * 2 + zl] = jnp.concatenate(
                    [q[zl * 32 : zl * 32 + 32, zh * 64 : zh * 64 + 64] for q in t], axis=1
                )
        for k in (3, 2, 4, 1, 5, 0, 6):
            z_copy(u, k).start()

    def f_copy(u, k):
        return remote(
            f_out.at[u, (g + 1 + k) % LINE], f_in.at[u * 3 + k], f_ss.at[u * 3 + k], f_rs.at[u * 3 + k], line_peer[k]
        )

    def power(u):
        for k in range(7):
            z_copy(u, k).wait_recv()
        t = z_out[u, z]
        for k in range(7):
            t = t + z_in[u * 7 + k]
        t = t * jnp.float32(2.0**-12)
        t = t * t
        t = t + pltpu.roll(t, 64, 1)
        for i in range(4):
            f_out[u, i] = t[i * 8 : i * 8 + 8]
        for k in range(3):
            f_copy(u, k).start()
        out_ref[(u // 2) * 4 + g, (u % 2) * 8 : (u % 2) * 8 + 8, :] = f_out[u, g][:, 0:64]

    def steer_alone(spec, cs):
        def some(i, carry):
            steer(i * 64, 64, spec, cs)
            return carry

        lax.fori_loop(0, 8, some, 0)

    steer_alone(a_spec(0, turns_0), cs_0)

    def a_pair(i, carry):
        s = i * 2

        @pl.when(i % 2 == 0)
        def _():
            load(i // 2).wait()

        a_dots(s, cs_0, a_spec(s + 1, turns_1), cs_1)

        @pl.when(i == 0)
        def _():
            pl.semaphore_wait(barrier, len(peers))
            for k in range(3):
                coord_copy(k).start()

        core_copy(s).start()

        @pl.when(i > 0)
        def _():
            finish(s - 1)

        a_dots(s + 1, cs_1, a_spec(jnp.minimum(s + 2, F - 1), turns_0), cs_0)
        core_copy(s + 1).start()

        finish(s)

        @pl.when(i == 3)
        def _():
            for k in range(3):
                coord_copy(k).wait_recv()
            steer_alone(b_spec(0, turns_2), cs_2)
            b_side(0, cs_2, b_spec(1, turns_3), cs_3)

        return carry

    lax.fori_loop(0, F // 2, a_pair, 0)
    finish(11)
    each(y_forward, 0, 1)
    b_side(1, cs_3, b_spec(2, turns_2), cs_2)
    each(z_send, 0, 1)
    each(y_forward, 2, 3)
    b_side(2, cs_2, None, None)
    each(z_send, 2, 3)
    each(power, 0, 1)
    each(y_forward, 4, 5)
    each(z_send, 4, 5)
    each(power, 2, 3)
    each(power, 4, 5)
    for u in range(UNITS):
        for k in range(3):
            f_copy(u, k).wait_recv()
            out_ref[(u // 2) * 4 + (g + 3 - k) % LINE, (u % 2) * 8 : (u % 2) * 8 + 8, :] = f_in[u * 3 + k][:, 0:64]

    def drain_core(s, carry):
        core_copy(s).wait_send()
        return carry

    lax.fori_loop(0, F, drain_core, 0)
    for k in range(3):
        coord_copy(k).wait_send()
    for k in range(9):
        line_copy(0, k, k % 3 + 1).wait_send()
    for u in range(UNITS):
        for d in range(2):
            for j in range(2):
                y1_copy(u, d, j).wait_send()
            y2_copy(u, d).wait_send()
        for k in range(7):
            z_copy(u, k).wait_send()
        for k in range(3):
            f_copy(u, k).wait_send()


def body(correlation, freq_bins, coords_a, coords_b, assign_a, assign_b, slow_a, slow_b):
    i32, f32, bf16 = jnp.int32, jnp.float32, jnp.bfloat16
    vmem = pl.BlockSpec(memory_space=pltpu.VMEM)
    dma = pltpu.SemaphoreType.DMA
    return pl.pallas_call(
        kernel,
        out_shape=jax.ShapeDtypeStruct((F, 16, 64), f32),
        in_specs=[pl.BlockSpec(memory_space=pl.ANY), pl.BlockSpec(memory_space=pltpu.SMEM)] + [vmem] * 6,
        out_specs=vmem,
        scratch_shapes=[
            pltpu.VMEM((2, F, 512, 128), bf16),
            pltpu.VMEM((64, 128), i32),
            pltpu.VMEM((64, 128), i32),
            pltpu.VMEM((8, 512), i32),
            pltpu.VMEM((8, 128), i32),
            pltpu.VMEM((2, 512, 128), i32),
            pltpu.VMEM((2, 512, 128), i32),
            pltpu.VMEM((1024, 256), bf16),
            pltpu.VMEM((512, 1024), bf16),
            pltpu.VMEM((512, 1024), bf16),
            pltpu.VMEM((512, 1024), bf16),
            pltpu.VMEM((512, 1024), bf16),
            pltpu.VMEM((8, 512), i32),
            pltpu.VMEM((8, 512), i32),
            pltpu.VMEM((8, 512), i32),
            pltpu.VMEM((8, 512), i32),
            pltpu.VMEM((F, 2, 256, 256), f32),
            pltpu.VMEM((F, 256, 256), f32),
            pltpu.VMEM((9, 256, 256), f32),
            pltpu.VMEM((3, 8, 128), i32),
            pltpu.VMEM((512, 1024), bf16),
            pltpu.VMEM((512, 1024), bf16),
            pltpu.VMEM((UNITS, 2, LINE, 64, 256), f32),
            pltpu.VMEM((UNITS, 2, 2, 64, 256), f32),
            pltpu.VMEM((UNITS, 2, 64, 256), f32),
            pltpu.VMEM((UNITS, 2, 64, 256), f32),
            pltpu.VMEM((UNITS, NZ, 32, 128), f32),
            pltpu.VMEM((UNITS * 7, 32, 128), f32),
            pltpu.VMEM((UNITS, LINE, 8, 128), f32),
            pltpu.VMEM((UNITS * 3, 8, 128), f32),
            dma((3,)),
            dma((F,)), dma((F,)),
            dma((9,)), dma((9,)),
            dma((3,)), dma((3,)),
            dma((UNITS * 4,)), dma((UNITS * 4,)),
            dma((UNITS * 2,)), dma((UNITS * 2,)),
            dma((UNITS * 7,)), dma((UNITS * 7,)),
            dma((UNITS * 3,)), dma((UNITS * 3,)),
        ],
        compiler_params=pltpu.CompilerParams(
            collective_id=0, has_side_effects=True, vmem_limit_bytes=56 * 2**20
        ),
        cost_estimate=pl.CostEstimate(flops=7 * 10**9, bytes_accessed=4 * 10**6, transcendentals=0),
    )(correlation, freq_bins, coords_a, coords_b, assign_a.reshape(1, 512), assign_b.reshape(1, 128), slow_a, slow_b)


def solution(mesh):
    return jax.shard_map(
        body,
        mesh=mesh,
        in_specs=(P(None, None, "arow", "bcol"), P(), P(), P(), P("arow"), P("bcol"), P(), P()),
        out_specs=P(None, "bcol", "arow"),
        check_vma=False,
    )
```

```python
import jax
import jax.numpy as jnp
from jax import lax
from jax.experimental import pallas as pl
from jax.experimental.pallas import tpu as pltpu
from jax.sharding import PartitionSpec as P

F = 12
ROUNDS = 3
UNITS = 6
LINE = 4
NZ = 8
MESH = pl.DeviceIdType.MESH

SIN = (4.442882834149931, -7.308241154546232, 3.6062889582237627, -0.8457635961366404, 0.10920575361787692)
COS = (1.4142134965650095, -6.978850988238499, 5.7394611706724765, -1.883562987243115, 0.3106981916942927)


def cos_sin(turns):
    r = turns.astype(jnp.float32) * jnp.float32(2.0**-32)
    u = r * r
    s = jnp.float32(SIN[4])
    c = jnp.float32(COS[4])
    for i in (3, 2, 1, 0):
        s = s * u + jnp.float32(SIN[i])
        c = c * u + jnp.float32(COS[i])
    s = s * r
    return 1.0 - s * s, s * c


def fraction(freq, place):
    product = freq * place
    return product * 83 + (product.astype(jnp.float32) * jnp.float32(0.88608)).astype(jnp.int32)


def places(coords_ref, assign, grid):
    for i in range(32):
        grid[2 * i : 2 * i + 2, :] = coords_ref[:, i * 128 : i * 128 + 128]
    table = grid[...]
    high = (table >> 8).astype(jnp.float32).astype(jnp.bfloat16)
    low = (table & 255).astype(jnp.float32).astype(jnp.bfloat16)
    n = assign.shape[1]
    lane = lax.broadcasted_iota(jnp.int32, (128, n), 0)
    pick = jnp.where(lane == (assign & 127), 1.0, 0.0).astype(jnp.bfloat16)
    value = 256.0 * jnp.dot(high, pick, preferred_element_type=jnp.float32) + jnp.dot(
        low, pick, preferred_element_type=jnp.float32
    )
    row = lax.broadcasted_iota(jnp.int32, (64, n), 0)
    value = jnp.where((row >> 1) == (assign >> 7), value, 0.0)
    px = jnp.sum(jnp.where((row & 1) == 0, value, 0.0), axis=0, keepdims=True)
    py = jnp.sum(jnp.where((row & 1) == 1, value, 0.0), axis=0, keepdims=True)
    return px.astype(jnp.int32), py.astype(jnp.int32)


def columns(slow_row):
    wide = jnp.broadcast_to(slow_row.astype(jnp.float32), (128, 128)).astype(jnp.bfloat16)
    i = lax.broadcasted_iota(jnp.int32, (128, 128), 0)
    j = lax.broadcasted_iota(jnp.int32, (128, 128), 1)
    eye = jnp.where(i == j, 1.0, 0.0).astype(jnp.bfloat16)
    out = lax.dot_general(eye, wide, (((1,), (1,)), ((), ())), preferred_element_type=jnp.float32)
    return out.astype(jnp.int32)


def kernel(corr_hbm, freq_ref, coords_a_ref, coords_b_ref, assign_a_ref, assign_b_ref, slow_a_ref, slow_b_ref, out_ref,
           corr_v, grid_a, grid_b, place_a, place_b, sa, sb, rhs, cs_0, cs_1, cs_2, cs_3, turns_0, turns_1, turns_2, turns_3, part, core_in, line_in, coord_in,
           v_hi, v_lo, y_part, y_in1, y_fwd, y_in2, z_out, z_in, f_out, f_in,
           corr_sem, core_ss, core_rs, line_ss, line_rs, coord_ss, coord_rs,
           y1_ss, y1_rs, y2_ss, y2_rs, z_ss, z_rs, f_ss, f_rs, z_known):
    arow = lax.axis_index("arow")
    bcol = lax.axis_index("bcol")
    core = arow % 2
    z = (arow // 2) * 2 + bcol % 2
    y = bcol // 8
    x = (bcol // 2) % 4
    g = x * (1 - core) + y * core
    h = y * (1 - core) + x * core

    def at(gg, hh, zz):
        xx = gg * (1 - core) + hh * core
        yy = hh * (1 - core) + gg * core
        return ((zz // 2) * 2 + core, (yy * 4 + xx) * 2 + zz % 2)

    near = h + 1 - 2 * (h % 2)
    wrap = 3 - h
    diagonal = 3 - near
    sibling = ((z // 2) * 2 + 1 - core, bcol)
    line_peer = [at((g + 1 + k) % LINE, h, z) for k in range(3)]
    z_peer = [at(g, h, (z + 1 + k) % NZ) for k in range(7)]

    def each(fn, *units):
        for u in units:
            fn(u)

    def load(r):
        four = pl.ds(r * 4, 4)
        return pltpu.make_async_copy(corr_hbm.at[:, four], corr_v.at[:, four], corr_sem.at[r])

    for r in range(ROUNDS):
        load(r).start()

    barrier = pltpu.get_barrier_semaphore()
    peers = [sibling, at(g, near, z), at(g, wrap, z)] + line_peer + [z_peer[0], z_peer[6]]
    for p in peers:
        pl.semaphore_signal(barrier, inc=1, device_id=p, device_id_type=MESH)

    bx, by = places(coords_b_ref, assign_b_ref[...], grid_b)
    place_b[...] = jnp.zeros_like(place_b)
    place_b[0:1, :] = bx
    place_b[1:2, :] = by
    ax, ay = places(coords_a_ref, assign_a_ref[...], grid_a)
    place_a[...] = jnp.zeros_like(place_a)
    place_a[0:1, :] = ax
    place_a[1:2, :] = ay
    for i in range(2):
        for t in range(4):
            c = columns(slow_a_ref[i : i + 1, t * 128 : t * 128 + 128])
            sa[i, t * 64 : t * 64 + 64, :] = c[0:64]
            sa[i, 256 + t * 64 : 256 + t * 64 + 64, :] = c[64:128]
            c = columns(slow_b_ref[i : i + 1, t * 128 : t * 128 + 128])
            for xx in range(4):
                gg = xx * (1 - core) + t * core
                hh = t * (1 - core) + xx * core
                for zl in range(2):
                    for half in range(2):
                        src = (xx * 2 + zl) * 16 + half * 8
                        dst = pl.multiple_of(half * 256 + hh * 64 + zl * 32 + gg * 8, 8)
                        sb[i, pl.ds(dst, 8), :] = c[src : src + 8]

    def remote(src, dst, ss, rs, dev):
        return pltpu.make_async_remote_copy(
            src_ref=src, dst_ref=dst, send_sem=ss, recv_sem=rs, device_id=dev, device_id_type=MESH
        )

    def coord_copy(k):
        return remote(place_b, coord_in.at[k], coord_ss.at[k], coord_rs.at[k], line_peer[k])

    def core_copy(s):
        return remote(part.at[s, 1 - core], core_in.at[s], core_ss.at[s], core_rs.at[s], sibling)

    def line_copy(s, slot, rel):
        return remote(
            part.at[s, core], line_in.at[slot], line_ss.at[slot], line_rs.at[slot], at((g + rel) % LINE, h, z)
        )

    def steer(start, count, spec, cs):
        s_ref, turns = spec
        xs = turns[0:1, :]
        ys = turns[1:2, :]
        for t in range(0, count, 16):
            rows = pl.ds(pl.multiple_of(start + t, 16), 16)
            s0 = s_ref[0, rows, :]
            s1 = s_ref[1, rows, :]
            s0 = jnp.concatenate([s0] * 4, axis=1)
            s1 = jnp.concatenate([s1] * 4, axis=1)
            c, s = cos_sin(s0 * xs + s1 * ys)
            cs[rows, 0:512] = c.astype(jnp.bfloat16)
            cs[rows, 512:1024] = s.astype(jnp.bfloat16)

    def a_bin(s):
        return (s // 4) * 4 + (x + y + 1 + s % 4) % LINE

    def a_spec(s, turns):
        turns[...] = fraction(freq_ref[a_bin(s)], place_a[...])
        return sa, turns

    def b_spec(r, turns):
        rows = [coord_in.at[0], coord_in.at[1], coord_in.at[2], place_b]
        turns[...] = fraction(freq_ref[r * 4 + g], jnp.concatenate([q[...] for q in rows], axis=1))
        return sb, turns

    def a_dots(s, cs, spec, cs_next):
        b = a_bin(s)
        cr = corr_v[0, b]
        ci = corr_v[1, b]
        rhs[0:512, 0:128] = cr
        rhs[0:512, 128:256] = ci
        rhs[512:1024, 0:128] = -ci
        rhs[512:1024, 128:256] = cr

        w = jnp.dot(cs[...], rhs[...], preferred_element_type=jnp.float32)
        part[s, 0] = w[0:256]
        part[s, 1] = w[256:512]
        steer(0, 512, spec, cs_next)

    def finish(s):
        core_copy(s).wait_recv()
        part[s, core] = part[s, core] + core_in[s]
        rel = (h + 1 + s % 4) % LINE

        @pl.when(rel > 0)
        def _():
            slot = (s // 4) * 3 + rel - 1

            line_copy(s, slot, rel).start()

    def pair(d):
        return (near, wrap) if d == 0 else (wrap, near)

    def y1_copy(u, d, j):
        first, _ = pair(d)
        block = diagonal if j == 0 else first
        i = (u * 2 + d) * 2 + j
        return remote(y_part.at[u, d, block], y_in1.at[u, d, j], y1_ss.at[i], y1_rs.at[i], at(g, first, z))

    def y2_copy(u, d):
        _, second = pair(d)
        return remote(y_fwd.at[u, d], y_in2.at[u, d], y2_ss.at[u * 2 + d], y2_rs.at[u * 2 + d], at(g, second, z))

    def b_side(r, cs, spec, cs_next):
        for k in range(4):
            if k < 3:
                line_copy(0, r * 3 + k, k + 1).wait_recv()
            w = line_in[r * 3 + k] if k < 3 else part[r * 4 + 3 - h, core]
            hi = w.astype(jnp.bfloat16)
            lo = (w - hi.astype(jnp.float32)).astype(jnp.bfloat16)
            re, im = slice(k * 128, k * 128 + 128), slice(512 + k * 128, 512 + k * 128 + 128)
            for dst, val in ((v_hi, hi), (v_lo, lo)):
                dst[0:256, re] = val[:, 0:128]
                dst[0:256, im] = val[:, 128:256]
                dst[256:512, re] = val[:, 128:256]
                dst[256:512, im] = -val[:, 0:128]

        dims = (((1,), (1,)), ((), ()))
        for d in range(2):
            part_d = slice(d * 256, d * 256 + 256)
            v = lax.dot_general(cs[...], v_hi[part_d, :], dims, preferred_element_type=jnp.float32)
            v = v + lax.dot_general(cs[...], v_lo[part_d, :], dims, preferred_element_type=jnp.float32)
            for half in range(2):
                for i in range(4):
                    y_part[r * 2 + half, d, i] = v[half * 256 + i * 64 : half * 256 + i * 64 + 64]
        if spec is not None:
            steer(0, 512, spec, cs_next)
        for half in range(2):
            for d in range(2):
                for j in range(2):
                    y1_copy(r * 2 + half, d, j).start()

    def z_tell(n):
        for d in range(2):
            pl.semaphore_signal(z_known.at[n * 2 + d], inc=1, device_id=z_peer[6 * d], device_id_type=MESH)

    def z_hear(n):
        for d in range(2):
            pl.semaphore_wait(z_known.at[n * 2 + d], 1)

    def y_forward(u):
        for d in range(2):
            _, second = pair(d)
            y1_copy(u, d, 0).wait_recv()
            y_fwd[u, d] = y_part[u, d, second] + y_in1[u, d, 0]
            y2_copy(u, d).start()

    def z_copy(u, k):
        return remote(
            z_out.at[u, (z + 1 + k) % NZ], z_in.at[u * 7 + k], z_ss.at[u * 7 + k], z_rs.at[u * 7 + k], z_peer[k]
        )

    def z_send(u):
        t = []
        for d in range(2):
            y1_copy(u, d, 1).wait_recv()
            y2_copy(u, d).wait_recv()
            t.append(y_part[u, d, h] + y_in1[u, d, 1] + y_in2[u, d])
        for zh in range(4):
            for zl in range(2):
                z_out[u, zh * 2 + zl] = jnp.concatenate(
                    [q[zl * 32 : zl * 32 + 32, zh * 64 : zh * 64 + 64] for q in t], axis=1
                )
        for k in (3, 2, 4, 1, 5, 0, 6):
            z_copy(u, k).start()

    def f_copy(u, k):
        return remote(
            f_out.at[u, (g + 1 + k) % LINE], f_in.at[u * 3 + k], f_ss.at[u * 3 + k], f_rs.at[u * 3 + k], line_peer[k]
        )

    def power(u):
        for k in range(7):
            z_copy(u, k).wait_recv()
        t = z_out[u, z]
        for k in range(7):
            t = t + z_in[u * 7 + k]
        t = t * jnp.float32(2.0**-12)
        t = t * t
        t = t + pltpu.roll(t, 64, 1)
        for i in range(4):
            f_out[u, i] = t[i * 8 : i * 8 + 8]
        for k in range(3):
            f_copy(u, k).start()
        out_ref[(u // 2) * 4 + g, (u % 2) * 8 : (u % 2) * 8 + 8, :] = f_out[u, g][:, 0:64]

    def steer_alone(spec, cs):
        def some(i, carry):
            steer(i * 64, 64, spec, cs)
            return carry

        lax.fori_loop(0, 8, some, 0)

    steer_alone(a_spec(0, turns_0), cs_0)

    def a_pair(i, carry):
        s = i * 2

        @pl.when(i % 2 == 0)
        def _():
            load(i // 2).wait()

        a_dots(s, cs_0, a_spec(s + 1, turns_1), cs_1)

        @pl.when(i == 0)
        def _():
            pl.semaphore_wait(barrier, len(peers))
            z_tell(0)
            for k in range(3):
                coord_copy(k).start()

        core_copy(s).start()

        @pl.when(i > 0)
        def _():
            finish(s - 1)

        a_dots(s + 1, cs_1, a_spec(jnp.minimum(s + 2, F - 1), turns_0), cs_0)
        core_copy(s + 1).start()

        finish(s)

        @pl.when(i == 3)
        def _():
            z_hear(0)
            z_tell(1)
            for k in range(3):
                coord_copy(k).wait_recv()
            steer_alone(b_spec(0, turns_2), cs_2)
            b_side(0, cs_2, b_spec(1, turns_3), cs_3)

        return carry

    lax.fori_loop(0, F // 2, a_pair, 0)
    z_hear(1)
    z_tell(2)
    finish(11)
    each(y_forward, 0, 1)
    b_side(1, cs_3, b_spec(2, turns_2), cs_2)
    z_hear(2)
    each(z_send, 0, 1)
    each(y_forward, 2, 3)
    b_side(2, cs_2, None, None)
    each(z_send, 2, 3)
    each(power, 0, 1)
    each(y_forward, 4, 5)
    each(z_send, 4, 5)
    each(power, 2, 3)
    each(power, 4, 5)
    for u in range(UNITS):
        for k in range(3):
            f_copy(u, k).wait_recv()
            out_ref[(u // 2) * 4 + (g + 3 - k) % LINE, (u % 2) * 8 : (u % 2) * 8 + 8, :] = f_in[u * 3 + k][:, 0:64]

    def drain_core(s, carry):
        core_copy(s).wait_send()
        return carry

    lax.fori_loop(0, F, drain_core, 0)
    for k in range(3):
        coord_copy(k).wait_send()
    for k in range(9):
        line_copy(0, k, k % 3 + 1).wait_send()
    for u in range(UNITS):
        for d in range(2):
            for j in range(2):
                y1_copy(u, d, j).wait_send()
            y2_copy(u, d).wait_send()
        for k in range(7):
            z_copy(u, k).wait_send()
        for k in range(3):
            f_copy(u, k).wait_send()


def body(correlation, freq_bins, coords_a, coords_b, assign_a, assign_b, slow_a, slow_b):
    i32, f32, bf16 = jnp.int32, jnp.float32, jnp.bfloat16
    vmem = pl.BlockSpec(memory_space=pltpu.VMEM)
    dma = pltpu.SemaphoreType.DMA
    return pl.pallas_call(
        kernel,
        out_shape=jax.ShapeDtypeStruct((F, 16, 64), f32),
        in_specs=[pl.BlockSpec(memory_space=pl.ANY), pl.BlockSpec(memory_space=pltpu.SMEM)] + [vmem] * 6,
        out_specs=vmem,
        scratch_shapes=[
            pltpu.VMEM((2, F, 512, 128), bf16),
            pltpu.VMEM((64, 128), i32),
            pltpu.VMEM((64, 128), i32),
            pltpu.VMEM((8, 512), i32),
            pltpu.VMEM((8, 128), i32),
            pltpu.VMEM((2, 512, 128), i32),
            pltpu.VMEM((2, 512, 128), i32),
            pltpu.VMEM((1024, 256), bf16),
            pltpu.VMEM((512, 1024), bf16),
            pltpu.VMEM((512, 1024), bf16),
            pltpu.VMEM((512, 1024), bf16),
            pltpu.VMEM((512, 1024), bf16),
            pltpu.VMEM((8, 512), i32),
            pltpu.VMEM((8, 512), i32),
            pltpu.VMEM((8, 512), i32),
            pltpu.VMEM((8, 512), i32),
            pltpu.VMEM((F, 2, 256, 256), f32),
            pltpu.VMEM((F, 256, 256), f32),
            pltpu.VMEM((9, 256, 256), f32),
            pltpu.VMEM((3, 8, 128), i32),
            pltpu.VMEM((512, 1024), bf16),
            pltpu.VMEM((512, 1024), bf16),
            pltpu.VMEM((UNITS, 2, LINE, 64, 256), f32),
            pltpu.VMEM((UNITS, 2, 2, 64, 256), f32),
            pltpu.VMEM((UNITS, 2, 64, 256), f32),
            pltpu.VMEM((UNITS, 2, 64, 256), f32),
            pltpu.VMEM((UNITS, NZ, 32, 128), f32),
            pltpu.VMEM((UNITS * 7, 32, 128), f32),
            pltpu.VMEM((UNITS, LINE, 8, 128), f32),
            pltpu.VMEM((UNITS * 3, 8, 128), f32),
            dma((3,)),
            dma((F,)), dma((F,)),
            dma((9,)), dma((9,)),
            dma((3,)), dma((3,)),
            dma((UNITS * 4,)), dma((UNITS * 4,)),
            dma((UNITS * 2,)), dma((UNITS * 2,)),
            dma((UNITS * 7,)), dma((UNITS * 7,)),
            dma((UNITS * 3,)), dma((UNITS * 3,)),
            pltpu.SemaphoreType.REGULAR((6,)),
        ],
        compiler_params=pltpu.CompilerParams(
            collective_id=0, has_side_effects=True, vmem_limit_bytes=56 * 2**20
        ),
        cost_estimate=pl.CostEstimate(flops=7 * 10**9, bytes_accessed=4 * 10**6, transcendentals=0),
    )(correlation, freq_bins, coords_a, coords_b, assign_a.reshape(1, 512), assign_b.reshape(1, 128), slow_a, slow_b)


def solution(mesh):
    return jax.shard_map(
        body,
        mesh=mesh,
        in_specs=(P(None, None, "arow", "bcol"), P(), P(), P(), P("arow"), P("bcol"), P(), P()),
        out_specs=P(None, "bcol", "arow"),
        check_vma=False,
    )
```
